32 devices in a mesh: fsdp: 8 (over y, x, core), rep: 4 (over z).
Axes of the slice: x: 2, y: 2, z: 4, core: 2. Of those that a mesh axis runs over, the one named last changes fastest.
Arguments:
- tokens: bfloat16 [16384, 1024], P(('fsdp', 'rep')), may hold values from -6 to 6
- seq_lengths: int32 [32, 4], P(('fsdp', 'rep')), may hold values from 1 to 320, 512 in all within a row
- attn_norm: bfloat16 [1024], P(('fsdp', 'rep')), may hold values from 0.25 to 1.75
- q_weight: bfloat16 [1024, 2048], P(('fsdp', 'rep')), may hold values from -0.1875 to 0.1875
- k_weight: bfloat16 [1024, 1024], P(('fsdp', 'rep')), may hold values from -0.1875 to 0.1875
- v_weight: bfloat16 [1024, 1024], P(('fsdp', 'rep')), may hold values from -0.1875 to 0.1875
- o_weight: bfloat16 [2048, 1024], P(('fsdp', 'rep')), may hold values from -1 to 1
- head_gains: bfloat16 [2, 128], replicated, may hold values from 0.25 to 1.75
- mlp_norm: bfloat16 [1024], P(('fsdp', 'rep')), may hold values from 0.25 to 1.75
- gate_weight: bfloat16 [1024, 3072], P(('fsdp', 'rep')), may hold values from -0.1875 to 0.1875
- up_weight: bfloat16 [1024, 3072], P(('fsdp', 'rep')), may hold values from -0.1875 to 0.1875
- down_weight: bfloat16 [3072, 1024], P(('fsdp', 'rep')), may hold values from -0.109375 to 0.109375
- cotangent: bfloat16 [16384, 1024], P(('fsdp', 'rep')), may hold values from -6 to 6
Outputs:
- layer_out: bfloat16 [16384, 1024], P(('fsdp', 'rep'))
- input_grad: float32 [16384, 1024], P(('fsdp', 'rep'))
- attn_norm_grad: float32 [1024], P(('fsdp', 'rep'))
- q_grad: float32 [1024, 2048], P(('fsdp', 'rep'))
- k_grad: float32 [1024, 1024], P(('fsdp', 'rep'))
- v_grad: float32 [1024, 1024], P(('fsdp', 'rep'))
- o_grad: float32 [2048, 1024], P(('fsdp', 'rep'))
- head_gains_grad: float32 [2, 128], replicated
- mlp_norm_grad: float32 [1024], P(('fsdp', 'rep'))
- gate_grad: float32 [1024, 3072], P(('fsdp', 'rep'))
- up_grad: float32 [1024, 3072], P(('fsdp', 'rep'))
- down_grad: float32 [3072, 1024], P(('fsdp', 'rep'))
The draws below stay inside these ranges and needn't reach their ends.
Inputs may be any that keep to these rules, and one draw needn't show every extreme that they name: `seq_lengths`: each row holds the lengths of the 4 sequences packed in order on one device; a row sums to 512, and its longest is exactly 320.
All inputs are finite; a program needn't handle non-finite values.
Results may differ from the reference program's by a relative error of at most 0.014.
Values may be sent and summed in bfloat16 or wider, within the bound.
A program may use at most 256 MiB of HBM per device.

```python
import math
import jax
import jax.numpy as jnp
import numpy as np
from jax import lax

D = 1024
HQ = 16
HK = 8
HD = 128
FF = 3072
TOK_DEV = 512
SEQS_DEV = 4
MOST_LEN = 320
TOKENS = 16384
N_FSDP = 8
N_REP = 4


def shard_levels(rng, shape, split, low, top_value):
    gain, own = 1.0, jax.random.fold_in(rng, 6)
    for dim, blocks in split:
        draws = jnp.exp(jax.random.uniform(jax.random.fold_in(own, dim), (blocks,), jnp.float32, low / len(split), top_value / len(split)))
        gain = gain * jnp.repeat(draws, shape[dim] // blocks).reshape([-1 if axis == dim else 1 for axis in range(len(shape))])
    return gain


def length_profile(number_of, total, reach, slope):
    weights = [(1 << 20) // math.isqrt(grade ** slope) + 1 for grade in range(2, number_of + 1)]
    spare, holding = total - reach - (number_of - 1), [1] * (number_of - 1)
    while spare > 0:
        free = [i for i in range(number_of - 1) if holding[i] < reach]
        whole, budget = sum([weights[i] for i in free]), spare
        for i in free:
            addition = min(reach - holding[i], max(1, budget * weights[i] // whole), spare)
            holding[i] = holding[i] + addition
            spare = spare - addition
    return np.array([reach] + holding)


def uneven_parts(own_key, count, total, limit, skew):
    if count == 2:
        one = jax.random.randint(own_key, (), max(1, total - limit), min(limit, total - 1) + 1)
        return jnp.stack([one, total - one])
    sizes = jnp.asarray(length_profile(count, total, limit, skew), jnp.int32)
    couples = (count - 1) // 2
    source_of, taker = sizes[1:1 + 2 * couples:2], sizes[2:2 + 2 * couples:2]
    room = jnp.minimum(source_of - 1, limit - taker)
    shifted = jax.random.randint(jax.random.fold_in(own_key, 1), (couples,), 0, 1 << 20) % (room + 1)
    sizes = sizes.at[1:1 + 2 * couples:2].set(source_of - shifted).at[2:2 + 2 * couples:2].set(taker + shifted)
    return sizes[jax.random.permutation(jax.random.fold_in(own_key, 2), count)]


def scatter_about(key, shape, spread, bound, split=(), held_as=jnp.bfloat16):
    result = jax.random.normal(key, shape, jnp.float32) * spread
    if len(split) > 0:
        result = shard_levels(key, shape, split, -0.22, 0.18) * result
    return jnp.clip(result, min=-bound, max=bound).astype(held_as)


def setup_inputs(seed: int = 0) -> dict:
    key_of = jax.random.split(jax.random.key(seed), 14)
    tokens = scatter_about(key_of[0], (TOKENS, D), 1.0, 6.0, ((0, 32),))
    seq_lengths = jax.vmap(lambda own: uneven_parts(own, SEQS_DEV, TOK_DEV, MOST_LEN, 2))(jax.random.split(key_of[1], (N_FSDP * N_REP))).reshape((N_FSDP * N_REP, SEQS_DEV)).astype(jnp.int32)
    attn_norm = jnp.clip(1.0 + 0.15 * jax.random.normal(key_of[2], (D,), jnp.float32), 0.25, 1.75).astype(jnp.bfloat16)
    q_weight = scatter_about(key_of[3], (D, HQ * HD), D ** -0.5, 0.1875, ((0, 32),))
    k_weight = scatter_about(key_of[4], (D, HK * HD), D ** -0.5, 0.1875, ((0, 32),))
    v_weight = scatter_about(key_of[5], (D, HK * HD), D ** -0.5, 0.1875, ((0, 32),))
    o_weight = scatter_about(key_of[6], (HQ * HD, D), (HQ * HD // 64) ** -0.5, 1.0, ((0, 32),))
    head_gains = jnp.clip(1.0 + 0.15 * jax.random.normal(key_of[7], (2, HD), jnp.float32), 0.25, 1.75).astype(jnp.bfloat16)
    mlp_norm = jnp.clip(1.0 + 0.15 * jax.random.normal(key_of[8], (D,), jnp.float32), 0.25, 1.75).astype(jnp.bfloat16)
    gate_weight = scatter_about(key_of[9], (D, FF), D ** -0.5, 0.1875, ((0, 32),))
    up_weight = scatter_about(key_of[10], (D, FF), D ** -0.5, 0.1875, ((0, 32),))
    down_weight = scatter_about(key_of[11], (FF, D), FF ** -0.5, 0.109375, ((0, 32),))
    cotangent = scatter_about(key_of[12], (TOKENS, D), 1.0, 6.0, ((0, 32),))
    return {"tokens": tokens, "seq_lengths": seq_lengths, "attn_norm": attn_norm, "q_weight": q_weight, "k_weight": k_weight, "v_weight": v_weight, "o_weight": o_weight, "head_gains": head_gains, "mlp_norm": mlp_norm, "gate_weight": gate_weight, "up_weight": up_weight, "down_weight": down_weight, "cotangent": cotangent}


EPSILON = 1e-06
ROPE_BASE = 1000000.0

@jax.custom_vjp
def low(v):
    return lax.optimization_barrier(v.astype(jnp.bfloat16)).astype(jnp.float32)

@jax.custom_vjp
def low_back(v):
    return v

def low_keep(v):
    return (low(v), None)

def low_pass(kept, grad):
    return (grad,)

def back_keep(v):
    return (v, None)

def back_low(kept, grad):
    return (low(grad),)
low.defvjp(low_keep, low_pass)
low_back.defvjp(back_keep, back_low)

def exact_dot(left, right):
    return jnp.dot(left, right, precision=lax.Precision.HIGHEST, preferred_element_type=jnp.float32)

def exact_einsum(form, left, right):
    return jnp.einsum(form, left, right, precision=lax.Precision.HIGHEST, preferred_element_type=jnp.float32)

def normalize(values, gain_row):
    return values * lax.rsqrt(lax.optimization_barrier(jnp.mean(values * values, axis=-1, keepdims=True)) + EPSILON) * gain_row

def rotary(values, cosine_table, sine_table):
    half_width = values.shape[-1] // 2
    first_half = values[..., :half_width]
    second_half = values[..., half_width:]
    return jnp.concatenate([first_half * cosine_table - second_half * sine_table, second_half * cosine_table + first_half * sine_table], axis=-1)

def layout(lengths_row, row_count):
    seq_ends = jnp.cumsum(lengths_row).astype(jnp.int32)
    seq_starts = (seq_ends - lengths_row).astype(jnp.int32)
    places = jnp.arange(row_count, dtype=jnp.int32)
    segment = lax.optimization_barrier(jnp.sum((places[:, None] >= seq_ends[None, :]).astype(jnp.int32), axis=1))
    owned_by = segment[:, None] == jnp.arange(lengths_row.shape[0], dtype=jnp.int32)[None, :]
    position = places - lax.optimization_barrier(jnp.sum(jnp.where(owned_by, seq_starts[None, :], 0), axis=1)).astype(jnp.int32)
    allowed = (segment[:, None] == segment[None, :]) & (places[None, :] <= places[:, None])
    return (position, allowed)

def layer(tokens, weights, lengths_row, product, batched):
    attn_norm, q_weight, k_weight, v_weight, o_weight, head_gains, mlp_norm, gate_weight, up_weight, down_weight = weights
    row_count = tokens.shape[0]
    head_size = head_gains.shape[1]
    kv_heads = k_weight.shape[1] // head_size
    q_heads = q_weight.shape[1] // head_size
    group_size = q_heads // kv_heads
    position, allowed = layout(lengths_row, row_count)
    frequency = ROPE_BASE ** (-(jnp.arange(head_size // 2, dtype=jnp.float32) * 2.0 / head_size))
    angles = position.astype(jnp.float32)[:, None] * frequency[None, :]
    cosine_table = jnp.cos(angles)[:, None, :]
    sine_table = jnp.sin(angles)[:, None, :]
    normed = low(normalize(tokens, attn_norm))
    queries = low_back(product(normed, q_weight)).reshape(row_count, q_heads, head_size)
    keys_raw = low_back(product(normed, k_weight)).reshape(row_count, kv_heads, head_size)
    values_in = low(low_back(product(normed, v_weight))).reshape(row_count, kv_heads, head_size)
    queries = low(rotary(normalize(queries, head_gains[0]), cosine_table, sine_table))
    keys = low(rotary(normalize(keys_raw, head_gains[1]), cosine_table, sine_table))
    query_groups = queries.reshape(row_count, kv_heads, group_size, head_size).transpose(1, 0, 2, 3)
    key_groups = keys.transpose(1, 0, 2)
    value_groups = values_in.transpose(1, 0, 2)

    def attend(operands):
        query_block, key_block, value_block = operands
        scores = batched('tgd,sd->gts', query_block, key_block) * head_size ** (-0.5)
        scores = low_back(scores)
        scores = jnp.where(allowed[None], scores, -1e+30)
        weights_soft = jnp.exp(scores - lax.optimization_barrier(jnp.max(scores, axis=-1, keepdims=True)))
        probabilities = low(weights_soft / lax.optimization_barrier(jnp.sum(weights_soft, axis=-1, keepdims=True)))
        return batched('gts,sd->tgd', probabilities, value_block)
    attended = lax.map(jax.checkpoint(attend), (query_groups, key_groups, value_groups))
    attended = attended.transpose(1, 0, 2, 3).reshape(row_count, q_heads * head_size)
    attended = low(low_back(attended))
    branch = low_back(product(attended, o_weight))
    middle = tokens + branch
    normed_two = low(normalize(middle, mlp_norm))
    gate_value = low_back(product(normed_two, gate_weight))
    up_value = low_back(product(normed_two, up_weight))
    hidden = low(jax.nn.silu(gate_value) * up_value)
    return middle + low_back(product(hidden, down_weight))

def reference(tokens, seq_lengths, attn_norm, q_weight, k_weight, v_weight, o_weight, head_gains, mlp_norm, gate_weight, up_weight, down_weight, cotangent):
    weights = tuple((item.astype(jnp.float32) for item in (attn_norm, q_weight, k_weight, v_weight, o_weight, head_gains, mlp_norm, gate_weight, up_weight, down_weight)))
    packs = N_FSDP * N_REP
    inputs = tokens.astype(jnp.float32).reshape(packs, TOK_DEV, D)

    def forward(pack_inputs, layer_weights):

        def one_pack(operands):
            return layer(operands[0], layer_weights, operands[1], exact_dot, exact_einsum)
        return lax.map(jax.checkpoint(one_pack), (pack_inputs, seq_lengths))
    outputs, pullback = jax.vjp(forward, inputs, weights)
    input_grad, weight_grads = pullback(cotangent.astype(jnp.float32).reshape(packs, TOK_DEV, D))
    return (outputs.reshape(TOKENS, D).astype(jnp.bfloat16), input_grad.reshape(TOKENS, D), weight_grads[0], weight_grads[1], weight_grads[2], weight_grads[3], weight_grads[4], weight_grads[5], weight_grads[6], weight_grads[7], weight_grads[8], weight_grads[9])
```

```python
import functools

import jax
import jax.numpy as jnp
from jax import lax
from jax.experimental import pallas as pl
from jax.experimental.pallas import tpu as pltpu
from jax.sharding import PartitionSpec as P

EPSILON = 1e-06
ROPE_BASE = 1000000.0
AXES = ("fsdp", "rep")
ROWS = 256


def low(values):
    return values.astype(jnp.bfloat16)


def high(values):
    return values.astype(jnp.float32)


def dot(left, right, dims):
    return lax.dot_general(left, right, (dims, ((), ())), preferred_element_type=jnp.float32)


NN = ((1,), (0,))
NT = ((1,), (1,))
TN = ((0,), (0,))


def gather(block):
    return lax.all_gather(block, AXES, axis=0, tiled=True)


def scatter_sum(values):
    return lax.psum_scatter(values, AXES, scatter_dimension=0, tiled=True)


def head_norm_rope(raw, gain, cosine, sine):
    rate = lax.rsqrt(jnp.mean(raw * raw, axis=-1, keepdims=True) + EPSILON)
    unit = raw * rate
    normed = unit * gain
    return unit, rate, low(normed * cosine + pltpu.roll(normed, raw.shape[1] // 2, 1) * sine)


def head_norm_rope_back(grad, unit, rate, gain, cosine, sine):
    grad = grad * cosine - pltpu.roll(grad, grad.shape[1] // 2, 1) * sine
    gain_grad = jnp.sum(grad * unit, axis=0, keepdims=True)
    scaled = grad * gain
    return rate * (scaled - unit * jnp.mean(unit * scaled, axis=-1, keepdims=True)), gain_grad


def probabilities(query, key, start, first, scale):
    scores = dot(query, key, NT) * scale
    row = lax.broadcasted_iota(jnp.int32, scores.shape, 0) + first
    column = lax.broadcasted_iota(jnp.int32, scores.shape, 1)
    scores = jnp.where((column <= row) & (column >= start), scores, -1e30)
    soft = jnp.exp(scores - jnp.max(scores, axis=-1, keepdims=True))
    return soft * (1.0 / jnp.sum(soft, axis=-1, keepdims=True))


def attention_kernel(group, qkv_ref, cosine_ref, sine_ref, gains_ref, start_ref, out_ref):
    size = gains_ref.shape[1]
    count = qkv_ref.shape[0]
    scale = size**-0.5
    cosine, sine = cosine_ref[...], sine_ref[...]
    key_at, value_at = group * size, (group + 1) * size
    key = head_norm_rope(qkv_ref[:, key_at:value_at], gains_ref[1:2], cosine, sine)[2]
    value = low(qkv_ref[:, value_at:])
    for head in range(group):
        span = slice(head * size, (head + 1) * size)
        query = head_norm_rope(qkv_ref[:, span], gains_ref[0:1], cosine, sine)[2]
        for first in range(0, count, ROWS):
            last = first + ROWS
            prob = probabilities(
                query[first:last], key[:last], start_ref[first:last], first, scale
            )
            out_ref[first:last, span] = low(dot(low(prob), value[:last], NN))


def attention_back_kernel(
    group,
    qkv_ref,
    cosine_ref,
    sine_ref,
    gains_ref,
    start_ref,
    out_ref,
    dout_ref,
    grad_ref,
    gain_grad_ref,
    dkey_ref,
    dvalue_ref,
    dquery_ref,
):
    size = gains_ref.shape[1]
    count = qkv_ref.shape[0]
    scale = size**-0.5
    cosine, sine = cosine_ref[...], sine_ref[...]
    key_at, value_at = group * size, (group + 1) * size

    @pl.when(pl.program_id(0) == 0)
    def _():
        gain_grad_ref[...] = jnp.zeros_like(gain_grad_ref)

    key_unit, key_rate, key = head_norm_rope(
        qkv_ref[:, key_at:value_at], gains_ref[1:2], cosine, sine
    )
    value = low(qkv_ref[:, value_at:])
    dkey_ref[...] = jnp.zeros_like(dkey_ref)
    dvalue_ref[...] = jnp.zeros_like(dvalue_ref)
    for head in range(group):
        span = slice(head * size, (head + 1) * size)
        query_unit, query_rate, query = head_norm_rope(
            qkv_ref[:, span], gains_ref[0:1], cosine, sine
        )
        dout = dout_ref[:, span]
        delta = jnp.sum(high(dout) * high(out_ref[:, span]), axis=-1, keepdims=True)
        for first in range(0, count, ROWS):
            last = first + ROWS
            prob = probabilities(
                query[first:last], key[:last], start_ref[first:last], first, scale
            )
            prob = low(prob)
            dprob = dot(dout[first:last], value[:last], NT)
            dscore = low(high(prob) * (dprob - delta[first:last]) * scale)
            dquery_ref[first:last] = dot(dscore, key[:last], NN)
            dkey_ref[:last] += dot(dscore, query[first:last], TN)
            dvalue_ref[:last] += dot(prob, dout[first:last], TN)
        dquery, gain_grad = head_norm_rope_back(
            dquery_ref[...], query_unit, query_rate, gains_ref[0:1], cosine, sine
        )
        grad_ref[:, span] = low(dquery)
        gain_grad_ref[0:1] += gain_grad
    dkey, gain_grad = head_norm_rope_back(
        dkey_ref[...], key_unit, key_rate, gains_ref[1:2], cosine, sine
    )
    grad_ref[:, key_at:value_at] = low(dkey)
    grad_ref[:, value_at:] = low(dvalue_ref[...])
    gain_grad_ref[1:2] += gain_grad


def attention_specs(count, size, width, wide):
    whole = lambda shape: pl.BlockSpec(shape, lambda step: (0, 0))
    return [
        pl.BlockSpec((count, wide), lambda step: (0, step)),
        whole((count, size)),
        whole((count, size)),
        whole((2, size)),
        whole((count, 1)),
    ]


def attention(qkv, cosine, sine, gains, start, group):
    count, size = cosine.shape
    wide = (group + 2) * size
    heads = qkv.shape[1] // wide
    return pl.pallas_call(
        functools.partial(attention_kernel, group),
        grid=(heads,),
        out_shape=jax.ShapeDtypeStruct((count, heads * group * size), jnp.bfloat16),
        in_specs=attention_specs(count, size, group, wide),
        out_specs=pl.BlockSpec((count, group * size), lambda step: (0, step)),
        compiler_params=pltpu.CompilerParams(vmem_limit_bytes=32 * 2**20),
        cost_estimate=pl.CostEstimate(
            flops=3 * heads * group * count * count * size,
            bytes_accessed=qkv.size * 4 + count * heads * group * size * 2,
            transcendentals=heads * group * count * count,
        ),
        name="attention",
    )(qkv, cosine, sine, gains, start)


def attention_back(qkv, cosine, sine, gains, start, out, dout, group):
    count, size = cosine.shape
    wide = (group + 2) * size
    heads = qkv.shape[1] // wide
    side = pl.BlockSpec((count, group * size), lambda step: (0, step))
    return pl.pallas_call(
        functools.partial(attention_back_kernel, group),
        grid=(heads,),
        out_shape=[
            jax.ShapeDtypeStruct(qkv.shape, jnp.bfloat16),
            jax.ShapeDtypeStruct((8, size), jnp.float32),
        ],
        in_specs=attention_specs(count, size, group, wide) + [side, side],
        out_specs=[
            pl.BlockSpec((count, wide), lambda step: (0, step)),
            pl.BlockSpec((8, size), lambda step: (0, 0)),
        ],
        scratch_shapes=[pltpu.VMEM((count, size), jnp.float32)] * 3,
        compiler_params=pltpu.CompilerParams(vmem_limit_bytes=32 * 2**20),
        cost_estimate=pl.CostEstimate(
            flops=8 * heads * group * count * count * size,
            bytes_accessed=qkv.size * 6 + count * heads * group * size * 4,
            transcendentals=heads * group * count * count,
        ),
        name="attention_back",
    )(qkv, cosine, sine, gains, start, out, dout)


def layout(lengths_row, row_count):
    ends = jnp.cumsum(lengths_row)
    places = jnp.arange(row_count, dtype=jnp.int32)
    passed = places[:, None] >= ends[None, :]
    return jnp.max(jnp.where(passed, ends[None, :], 0), axis=1)


def rates(values):
    return lax.rsqrt(jnp.mean(values * values, axis=-1, keepdims=True) + EPSILON)


def norm_back(values, rate, gain, grad):
    scaled = grad * gain
    mean = jnp.mean(values * scaled, axis=-1, keepdims=True)
    gain_grad = jnp.sum(grad * values * rate, axis=0)
    return rate * scaled - values * (rate * rate * rate) * mean, gain_grad


def grouped(q_part, k_part, v_part, kv_heads):
    rows = q_part.shape[0]
    parts = [item.reshape(rows, kv_heads, -1) for item in (q_part, k_part, v_part)]
    return jnp.concatenate(parts, axis=2).reshape(rows, -1)


def local(
    tokens,
    seq_lengths,
    attn_norm,
    q_weight,
    k_weight,
    v_weight,
    o_weight,
    head_gains,
    mlp_norm,
    gate_weight,
    up_weight,
    down_weight,
    cotangent,
):
    count = tokens.shape[0]
    size = head_gains.shape[1]
    kv_heads = k_weight.shape[1] // size
    group = q_weight.shape[1] // k_weight.shape[1]
    hidden = gate_weight.shape[1]
    own = attn_norm.shape[0]

    norms = gather(jnp.stack([attn_norm, mlp_norm], axis=1))
    gain_one, gain_two = high(norms[:, 0]), high(norms[:, 1])
    qkv_weight = gather(grouped(q_weight, k_weight, v_weight, kv_heads))
    out_weight = gather(o_weight)
    pair_weight = gather(jnp.concatenate([gate_weight, up_weight], axis=1))
    back_weight = gather(down_weight)

    start = layout(seq_lengths[0], count)
    position = jnp.arange(count, dtype=jnp.int32) - start
    frequency = ROPE_BASE ** (-(jnp.arange(size // 2, dtype=jnp.float32) * 2.0 / size))
    angles = position.astype(jnp.float32)[:, None] * frequency[None, :]
    cosine, sine = jnp.cos(angles), jnp.sin(angles)
    cosine = jnp.concatenate([cosine, cosine], axis=1)
    sine = jnp.concatenate([-sine, sine], axis=1)
    gains = high(head_gains)
    tables = (cosine, sine, gains, start[:, None])

    inputs = high(tokens)
    rate_one = rates(inputs)
    normed_one = low(inputs * rate_one * gain_one)
    qkv = dot(normed_one, qkv_weight, NN)
    attended = attention(qkv, *tables, group)
    middle = inputs + dot(attended, out_weight, NN)
    rate_two = rates(middle)
    normed_two = low(middle * rate_two * gain_two)
    pair = dot(normed_two, pair_weight, NN)
    gate, up = pair[:, :hidden], pair[:, hidden:]
    gate_sigmoid = jax.nn.sigmoid(gate)
    gate_silu = gate * gate_sigmoid
    mixed = low(gate_silu * up)
    layer_out = low(middle + dot(mixed, back_weight, NN))

    down_sum = scatter_sum(low(dot(mixed, cotangent, TN)))
    dmixed = dot(cotangent, back_weight, NT)
    dgate = low(dmixed * up * (gate_sigmoid + gate_silu * (1.0 - gate_sigmoid)))
    dup = low(dmixed * gate_silu)
    dpair = jnp.concatenate([dgate, dup], axis=1)
    pair_sum = scatter_sum(low(dot(normed_two, dpair, TN)))
    dnormed_two = dot(dpair, pair_weight, NT)
    dmiddle, mlp_norm_grad = norm_back(middle, rate_two, gain_two, dnormed_two)
    dmiddle = high(cotangent) + dmiddle
    dbranch = low(dmiddle)
    out_sum = scatter_sum(low(dot(attended, dbranch, TN)))
    dattended = low(dot(dbranch, out_weight, NT))
    dqkv, gains_grad = attention_back(qkv, *tables, attended, dattended, group)
    qkv_sum = scatter_sum(low(dot(normed_one, dqkv, TN)))
    dnormed_one = dot(dqkv, qkv_weight, NT)
    dinputs, attn_norm_grad = norm_back(inputs, rate_one, gain_one, dnormed_one)
    input_grad = dmiddle + dinputs

    small = lax.psum(
        jnp.concatenate([attn_norm_grad, mlp_norm_grad, gains_grad[:2].reshape(-1)]), AXES
    )
    width = attn_norm_grad.shape[0]
    place = (lax.axis_index("fsdp") * lax.axis_size("rep") + lax.axis_index("rep")) * own
    attn_norm_sum = lax.dynamic_slice(small, (place,), (own,))
    mlp_norm_sum = lax.dynamic_slice(small, (width + place,), (own,))
    gains_sum = small[2 * width :].reshape(2, size)

    qkv_sum = high(qkv_sum).reshape(own, kv_heads, -1)
    q_sum = qkv_sum[:, :, : group * size].reshape(own, -1)
    k_sum = qkv_sum[:, :, group * size : (group + 1) * size].reshape(own, -1)
    v_sum = qkv_sum[:, :, (group + 1) * size :].reshape(own, -1)
    pair_sum = high(pair_sum)
    return (
        layer_out,
        input_grad,
        attn_norm_sum,
        q_sum,
        k_sum,
        v_sum,
        high(out_sum),
        gains_sum,
        mlp_norm_sum,
        pair_sum[:, :hidden],
        pair_sum[:, hidden:],
        high(down_sum),
    )


def solution(mesh):
    split, line = P(AXES, None), P(AXES)
    return jax.shard_map(
        local,
        mesh=mesh,
        in_specs=(
            split, split, line, split, split, split, split, P(), line, split, split, split, split
        ),
        out_specs=(
            split, split, line, split, split, split, split, P(), line, split, split, split
        ),
        check_vma=False,
    )
```

```python
import functools

import jax
import jax.numpy as jnp
from jax import lax
from jax.experimental import pallas as pl
from jax.experimental.pallas import tpu as pltpu
from jax.sharding import PartitionSpec as P

EPSILON = 1e-06
ROPE_BASE = 1000000.0
AXES = ("fsdp", "rep")
ROWS = 256


def low(values):
    return values.astype(jnp.bfloat16)


def high(values):
    return values.astype(jnp.float32)


def dot(left, right, dims):
    return lax.dot_general(left, right, (dims, ((), ())), preferred_element_type=jnp.float32)


NN = ((1,), (0,))
NT = ((1,), (1,))
TN = ((0,), (0,))


def gather(block):
    return lax.all_gather(block, AXES, axis=0, tiled=True)


def mesh_bits():
    bits = []
    for axis in AXES:
        step = lax.axis_size(axis) // 2
        while step > 0:
            bits.append((axis, step))
            step //= 2
    return bits


def swap(values, axis, step):
    pairs = [(here, here ^ step) for here in range(lax.axis_size(axis))]
    return lax.ppermute(values, axis, pairs)


def bit_of(axis, step):
    return (lax.axis_index(axis) // step) % 2


def exchange_order(turn):
    bits = mesh_bits()
    last = [bit for bit in bits if bit[0] == AXES[1] and bit[1] > 1]
    middle = [bit for bit in bits if bit not in last and bit != (AXES[0], 1)]
    turn = turn % len(middle)
    return [(AXES[0], 1)] + middle[turn:] + middle[:turn] + last


def scatter_sum(values, turn):
    left = mesh_bits()
    order = exchange_order(turn)
    width = values.shape[1]
    for axis, step in order:
        place = left.index((axis, step))
        left.remove((axis, step))
        halves = values.reshape(2**place, 2, -1, width)
        bit = bit_of(axis, step)
        mine = lax.dynamic_index_in_dim(halves, bit, 1, keepdims=False)
        other = lax.dynamic_index_in_dim(halves, 1 - bit, 1, keepdims=False)
        total = high(mine) + high(swap(other, axis, step))
        values = low(total) if left else total
        values = values.reshape(-1, width)
    return values


def sum_all(values):
    for axis, step in mesh_bits():
        values = values + swap(values, axis, step)
    return values


def head_norm_rope(raw, gain, cosine, sine):
    rate = lax.rsqrt(jnp.mean(raw * raw, axis=-1, keepdims=True) + EPSILON)
    unit = raw * rate
    normed = unit * gain
    return unit, rate, low(normed * cosine + pltpu.roll(normed, raw.shape[1] // 2, 1) * sine)


def head_norm_rope_back(grad, unit, rate, gain, cosine, sine):
    grad = grad * cosine - pltpu.roll(grad, grad.shape[1] // 2, 1) * sine
    gain_grad = jnp.sum(grad * unit, axis=0, keepdims=True)
    scaled = grad * gain
    return rate * (scaled - unit * jnp.mean(unit * scaled, axis=-1, keepdims=True)), gain_grad


def probabilities(query, key, start, first, scale):
    scores = dot(query, key, NT) * scale
    row = lax.broadcasted_iota(jnp.int32, scores.shape, 0) + first
    column = lax.broadcasted_iota(jnp.int32, scores.shape, 1)
    scores = jnp.where((column <= row) & (column >= start), scores, -1e30)
    soft = jnp.exp(scores - jnp.max(scores, axis=-1, keepdims=True))
    return soft * (1.0 / jnp.sum(soft, axis=-1, keepdims=True))


def attention_kernel(group, qkv_ref, cosine_ref, sine_ref, gains_ref, start_ref, out_ref):
    size = gains_ref.shape[1]
    count = qkv_ref.shape[0]
    scale = size**-0.5
    cosine, sine = cosine_ref[...], sine_ref[...]
    key_at, value_at = group * size, (group + 1) * size
    key = head_norm_rope(qkv_ref[:, key_at:value_at], gains_ref[1:2], cosine, sine)[2]
    value = low(qkv_ref[:, value_at:])
    for head in range(group):
        span = slice(head * size, (head + 1) * size)
        query = head_norm_rope(qkv_ref[:, span], gains_ref[0:1], cosine, sine)[2]
        for first in range(0, count, ROWS):
            last = first + ROWS
            prob = probabilities(
                query[first:last], key[:last], start_ref[first:last], first, scale
            )
            out_ref[first:last, span] = low(dot(low(prob), value[:last], NN))


def attention_back_kernel(
    group,
    qkv_ref,
    cosine_ref,
    sine_ref,
    gains_ref,
    start_ref,
    out_ref,
    dout_ref,
    grad_ref,
    gain_grad_ref,
    dkey_ref,
    dvalue_ref,
    dquery_ref,
):
    size = gains_ref.shape[1]
    count = qkv_ref.shape[0]
    scale = size**-0.5
    cosine, sine = cosine_ref[...], sine_ref[...]
    key_at, value_at = group * size, (group + 1) * size

    @pl.when(pl.program_id(0) == 0)
    def _():
        gain_grad_ref[...] = jnp.zeros_like(gain_grad_ref)

    key_unit, key_rate, key = head_norm_rope(
        qkv_ref[:, key_at:value_at], gains_ref[1:2], cosine, sine
    )
    value = low(qkv_ref[:, value_at:])
    dkey_ref[...] = jnp.zeros_like(dkey_ref)
    dvalue_ref[...] = jnp.zeros_like(dvalue_ref)
    for head in range(group):
        span = slice(head * size, (head + 1) * size)
        query_unit, query_rate, query = head_norm_rope(
            qkv_ref[:, span], gains_ref[0:1], cosine, sine
        )
        dout = dout_ref[:, span]
        delta = jnp.sum(high(dout) * high(out_ref[:, span]), axis=-1, keepdims=True)
        for first in range(0, count, ROWS):
            last = first + ROWS
            prob = probabilities(
                query[first:last], key[:last], start_ref[first:last], first, scale
            )
            prob = low(prob)
            dprob = dot(dout[first:last], value[:last], NT)
            dscore = low(high(prob) * (dprob - delta[first:last]) * scale)
            dquery_ref[first:last] = dot(dscore, key[:last], NN)
            dkey_ref[:last] += dot(dscore, query[first:last], TN)
            dvalue_ref[:last] += dot(prob, dout[first:last], TN)
        dquery, gain_grad = head_norm_rope_back(
            dquery_ref[...], query_unit, query_rate, gains_ref[0:1], cosine, sine
        )
        grad_ref[:, span] = low(dquery)
        gain_grad_ref[0:1] += gain_grad
    dkey, gain_grad = head_norm_rope_back(
        dkey_ref[...], key_unit, key_rate, gains_ref[1:2], cosine, sine
    )
    grad_ref[:, key_at:value_at] = low(dkey)
    grad_ref[:, value_at:] = low(dvalue_ref[...])
    gain_grad_ref[1:2] += gain_grad


def attention_specs(count, size, width, wide):
    whole = lambda shape: pl.BlockSpec(shape, lambda step: (0, 0))
    return [
        pl.BlockSpec((count, wide), lambda step: (0, step)),
        whole((count, size)),
        whole((count, size)),
        whole((2, size)),
        whole((count, 1)),
    ]


def attention(qkv, cosine, sine, gains, start, group):
    count, size = cosine.shape
    wide = (group + 2) * size
    heads = qkv.shape[1] // wide
    return pl.pallas_call(
        functools.partial(attention_kernel, group),
        grid=(heads,),
        out_shape=jax.ShapeDtypeStruct((count, heads * group * size), jnp.bfloat16),
        in_specs=attention_specs(count, size, group, wide),
        out_specs=pl.BlockSpec((count, group * size), lambda step: (0, step)),
        compiler_params=pltpu.CompilerParams(vmem_limit_bytes=32 * 2**20),
        cost_estimate=pl.CostEstimate(
            flops=3 * heads * group * count * count * size,
            bytes_accessed=qkv.size * 4 + count * heads * group * size * 2,
            transcendentals=heads * group * count * count,
        ),
        name="attention",
    )(qkv, cosine, sine, gains, start)


def attention_back(qkv, cosine, sine, gains, start, out, dout, group):
    count, size = cosine.shape
    wide = (group + 2) * size
    heads = qkv.shape[1] // wide
    side = pl.BlockSpec((count, group * size), lambda step: (0, step))
    return pl.pallas_call(
        functools.partial(attention_back_kernel, group),
        grid=(heads,),
        out_shape=[
            jax.ShapeDtypeStruct(qkv.shape, jnp.bfloat16),
            jax.ShapeDtypeStruct((8, size), jnp.float32),
        ],
        in_specs=attention_specs(count, size, group, wide) + [side, side],
        out_specs=[
            pl.BlockSpec((count, wide), lambda step: (0, step)),
            pl.BlockSpec((8, size), lambda step: (0, 0)),
        ],
        scratch_shapes=[pltpu.VMEM((count, size), jnp.float32)] * 3,
        compiler_params=pltpu.CompilerParams(vmem_limit_bytes=32 * 2**20),
        cost_estimate=pl.CostEstimate(
            flops=8 * heads * group * count * count * size,
            bytes_accessed=qkv.size * 6 + count * heads * group * size * 4,
            transcendentals=heads * group * count * count,
        ),
        name="attention_back",
    )(qkv, cosine, sine, gains, start, out, dout)


def layout(lengths_row, row_count):
    ends = jnp.cumsum(lengths_row)
    places = jnp.arange(row_count, dtype=jnp.int32)
    passed = places[:, None] >= ends[None, :]
    return jnp.max(jnp.where(passed, ends[None, :], 0), axis=1)


def rates(values):
    return lax.rsqrt(jnp.mean(values * values, axis=-1, keepdims=True) + EPSILON)


def norm_back(values, rate, gain, grad):
    scaled = grad * gain
    mean = jnp.mean(values * scaled, axis=-1, keepdims=True)
    gain_grad = jnp.sum(grad * values * rate, axis=0)
    return rate * scaled - values * (rate * rate * rate) * mean, gain_grad


def grouped(q_part, k_part, v_part, kv_heads):
    rows = q_part.shape[0]
    parts = [item.reshape(rows, kv_heads, -1) for item in (q_part, k_part, v_part)]
    return jnp.concatenate(parts, axis=2).reshape(rows, -1)


def local(
    tokens,
    seq_lengths,
    attn_norm,
    q_weight,
    k_weight,
    v_weight,
    o_weight,
    head_gains,
    mlp_norm,
    gate_weight,
    up_weight,
    down_weight,
    cotangent,
):
    count = tokens.shape[0]
    size = head_gains.shape[1]
    kv_heads = k_weight.shape[1] // size
    group = q_weight.shape[1] // k_weight.shape[1]
    hidden = gate_weight.shape[1]
    own = attn_norm.shape[0]

    norms = gather(jnp.stack([attn_norm, mlp_norm], axis=1))
    gain_one, gain_two = high(norms[:, 0]), high(norms[:, 1])
    qkv_weight = gather(grouped(q_weight, k_weight, v_weight, kv_heads))
    out_weight = gather(o_weight)
    pair_weight = gather(jnp.concatenate([gate_weight, up_weight], axis=1))
    back_weight = gather(down_weight)

    start = layout(seq_lengths[0], count)
    position = jnp.arange(count, dtype=jnp.int32) - start
    frequency = ROPE_BASE ** (-(jnp.arange(size // 2, dtype=jnp.float32) * 2.0 / size))
    angles = position.astype(jnp.float32)[:, None] * frequency[None, :]
    cosine, sine = jnp.cos(angles), jnp.sin(angles)
    cosine = jnp.concatenate([cosine, cosine], axis=1)
    sine = jnp.concatenate([-sine, sine], axis=1)
    gains = high(head_gains)
    tables = (cosine, sine, gains, start[:, None])

    inputs = high(tokens)
    rate_one = rates(inputs)
    normed_one = low(inputs * rate_one * gain_one)
    qkv = dot(normed_one, qkv_weight, NN)
    attended = attention(qkv, *tables, group)
    middle = inputs + dot(attended, out_weight, NN)
    rate_two = rates(middle)
    normed_two = low(middle * rate_two * gain_two)
    pair = dot(normed_two, pair_weight, NN)
    gate, up = pair[:, :hidden], pair[:, hidden:]
    gate_sigmoid = jax.nn.sigmoid(gate)
    gate_silu = gate * gate_sigmoid
    mixed = low(gate_silu * up)
    layer_out = low(middle + dot(mixed, back_weight, NN))

    down_sum = scatter_sum(low(dot(mixed, cotangent, TN)), 0)
    dmixed = dot(cotangent, back_weight, NT)
    dgate = low(dmixed * up * (gate_sigmoid + gate_silu * (1.0 - gate_sigmoid)))
    dup = low(dmixed * gate_silu)
    gate_sum = scatter_sum(low(dot(normed_two, dgate, TN)), 1)
    up_sum = scatter_sum(low(dot(normed_two, dup, TN)), 2)
    dpair = jnp.concatenate([dgate, dup], axis=1)
    dnormed_two = dot(dpair, pair_weight, NT)
    dmiddle, mlp_norm_grad = norm_back(middle, rate_two, gain_two, dnormed_two)
    dmiddle = high(cotangent) + dmiddle
    dbranch = low(dmiddle)
    out_sum = scatter_sum(low(dot(attended, dbranch, TN)), 0)
    dattended = low(dot(dbranch, out_weight, NT))
    dqkv, gains_grad = attention_back(qkv, *tables, attended, dattended, group)
    half = dqkv.shape[1] // 2
    qkv_sum = jnp.concatenate(
        [
            scatter_sum(low(dot(normed_one, dqkv[:, :half], TN)), 1),
            scatter_sum(low(dot(normed_one, dqkv[:, half:], TN)), 2),
        ],
        axis=1,
    )
    dnormed_one = dot(dqkv, qkv_weight, NT)
    dinputs, attn_norm_grad = norm_back(inputs, rate_one, gain_one, dnormed_one)
    input_grad = dmiddle + dinputs

    small = sum_all(
        jnp.concatenate([attn_norm_grad, mlp_norm_grad, gains_grad[:2].reshape(-1)])
    )
    width = attn_norm_grad.shape[0]
    place = (lax.axis_index("fsdp") * lax.axis_size("rep") + lax.axis_index("rep")) * own
    attn_norm_sum = lax.dynamic_slice(small, (place,), (own,))
    mlp_norm_sum = lax.dynamic_slice(small, (width + place,), (own,))
    gains_sum = small[2 * width :].reshape(2, size)

    qkv_sum = qkv_sum.reshape(own, kv_heads, -1)
    q_sum = qkv_sum[:, :, : group * size].reshape(own, -1)
    k_sum = qkv_sum[:, :, group * size : (group + 1) * size].reshape(own, -1)
    v_sum = qkv_sum[:, :, (group + 1) * size :].reshape(own, -1)
    return (
        layer_out,
        input_grad,
        attn_norm_sum,
        q_sum,
        k_sum,
        v_sum,
        out_sum,
        gains_sum,
        mlp_norm_sum,
        gate_sum,
        up_sum,
        down_sum,
    )


def solution(mesh):
    split, line = P(AXES, None), P(AXES)
    return jax.shard_map(
        local,
        mesh=mesh,
        in_specs=(
            split, split, line, split, split, split, split, P(), line, split, split, split, split
        ),
        out_specs=(
            split, split, line, split, split, split, split, P(), line, split, split, split
        ),
        check_vma=False,
    )
```
